512 devices in a mesh: seq: 32 (over x, y_lo, core), chan: 16 (over y_hi, z).
Axes of the slice: x: 4, y: 8 (y_hi: 2, y_lo: 4; y = y_hi * 4 + y_lo), z: 8, core: 2. Of those that a mesh axis runs over, the one named last changes fastest.
Arguments:
- key_value: bfloat16 [16384, 4096], P('seq', 'chan'), may hold values from -6 to 6
- gating: bfloat16 [16384, 4096], P('seq', 'chan'), may hold values from -6 to 6
- long_filter: bfloat16 [16384, 4096], P('seq', 'chan'), may hold values from -0.046875 to 0.046875
- skip_gain: float32 [4096], P('chan'), may hold values from -4 to 4
- out_weight: bfloat16 [4096, 4096], P('chan'), may hold values from -0.125 to 0.125
Outputs:
- mixed: bfloat16 [16384, 4096], P('seq', 'chan')
The draws below stay inside these ranges and needn't reach their ends.
All inputs are finite; a program needn't handle non-finite values.
Results may differ from the reference program's by a relative error of at most 0.023.
Values may be sent and summed in bfloat16 or wider, within the bound.
A program may use at most 64 MiB of HBM per device.

```python
import jax
import jax.numpy as jnp
from jax import lax

CH_DEV = 256
D_OUT = 4096
TOKENS = 16384
CHANNELS = 4096


def spiked(result, own_key, source, target, parts, factor):
    owner, partner = [(jnp.arange(result.shape[dim]) // (result.shape[dim] // parts)).reshape([-1 if axis == dim else 1 for axis in range(result.ndim)]) for dim in (source, target)]
    chosen = jax.random.permutation(own_key, parts)[partner]
    strong = (owner == chosen) | (owner == (partner + parts // 2) % parts)
    return jnp.where(strong, factor * result, result)


def block_levels(key, extent, cuts, smallest, top_value):
    def one(axis_at, shards_of):
        heights = jax.random.uniform(jax.random.fold_in(jax.random.fold_in(key, 6), axis_at), (shards_of,), jnp.float32, smallest / len(cuts), top_value / len(cuts))
        return jnp.repeat(jnp.exp(heights), extent[axis_at] // shards_of).reshape((-1,) + (1,) * (len(extent) - axis_at - 1))

    level = one(*cuts[0])
    for cut in cuts[1:]:
        level = level * one(*cut)
    return level


def normal_values(key, shape, scale, bound, split=(), kind=jnp.bfloat16):
    level = block_levels(key, shape, split, -0.22, 0.18) if split else 1.0
    values = jax.random.normal(key, shape, jnp.float32) * scale * level
    return jnp.minimum(jnp.maximum(values, -bound), bound).astype(kind)


def heavy_noise(own_key, shape, spread, bound, pieces, heavy, kind=jnp.bfloat16):
    drawn = spread * jax.random.normal(own_key, shape, jnp.float32)
    if pieces:
        drawn = drawn * block_levels(own_key, shape, pieces, -0.22, 0.18)
    return jnp.clip(spiked(drawn, jax.random.fold_in(own_key, 3), *heavy), -bound, bound).astype(kind)


def setup_inputs(seed: int = 0) -> dict:
    key_of = jax.random.split(jax.random.key(seed), 6)
    return {
        "key_value": normal_values(key_of[0], (TOKENS, CHANNELS), 1.0, 6.0, ((0, 32), (1, 16))),
        "gating": normal_values(key_of[1], (TOKENS, CHANNELS), 1.0, 6.0, ((0, 32), (1, 16))),
        "long_filter": normal_values(key_of[2], (TOKENS, CHANNELS), TOKENS ** -0.5, 0.046875, ((0, 32), (1, 16))),
        "skip_gain": normal_values(key_of[3], (CHANNELS,), 1.0, 4.0, ((0, 16),), jnp.float32),
        "out_weight": heavy_noise(key_of[4], (CHANNELS, D_OUT), CHANNELS ** -0.5, 0.125, ((0, 16),), (0, 1, 16, 2.0)),
    }


def reference(key_value, gating, long_filter, skip_gain, out_weight):
    length = TOKENS
    groups = CHANNELS // CH_DEV
    signal = key_value.astype(jnp.float32)
    kernel = long_filter.astype(jnp.float32)

    def convolve_group(pair):
        group_signal, group_kernel = pair
        signal_freq = jnp.fft.rfft(group_signal, n=2 * length, axis=0)
        kernel_freq = jnp.fft.rfft(group_kernel, n=2 * length, axis=0)
        return jnp.fft.irfft(signal_freq * kernel_freq, n=2 * length, axis=0)[:length]

    split_signal = signal.reshape(length, groups, CH_DEV).transpose(1, 0, 2)
    split_kernel = kernel.reshape(length, groups, CH_DEV).transpose(1, 0, 2)
    conv = lax.map(convolve_group, (split_signal, split_kernel))
    conv = conv.transpose(1, 0, 2).reshape(length, CHANNELS)
    gated = (gating.astype(jnp.float32) * (conv + skip_gain[None, :] * signal)).astype(jnp.bfloat16)
    split_gated = gated.reshape(length, groups, CH_DEV).transpose(1, 0, 2)
    split_weight = out_weight.reshape(groups, CH_DEV, D_OUT)

    def add_group(total, pair):
        group_gated, group_weight = pair
        partial_value = jnp.dot(group_gated, group_weight, preferred_element_type=jnp.float32).astype(jnp.bfloat16)
        partial_value = lax.optimization_barrier(partial_value)
        return total + partial_value.astype(jnp.float32), None

    start = jnp.zeros((length, D_OUT), jnp.float32)
    total, unused = lax.scan(add_group, start, (split_gated, split_weight))
    return total.astype(jnp.bfloat16)
```

```python
import functools

import jax
import jax.numpy as jnp
import ml_dtypes
import numpy as np
from jax import lax
from jax.experimental import pallas as pl
from jax.experimental.pallas import tpu as pltpu
from jax.sharding import PartitionSpec as P

MESH = pl.DeviceIdType.MESH
F32 = jnp.float32
BF16 = jnp.bfloat16
SEQ = 32
Z = 8
LANES = 128
TOK = 512
CH = 256
SEGS = TOK // LANES
HALVES = 2
CHUNK_CH = CH // HALVES
OWN = CHUNK_CH // SEQ
ROWS = OWN * SEGS
TOK_CHUNKS = 4
PIECE = TOK // TOK_CHUNKS
SHARE = 32
SHARES = CH // SHARE


def tables():
    freq = (2 * np.arange(128) + 1) * np.pi / 256
    angle = np.arange(256)[:, None] * freq[None, :]
    both = np.concatenate([np.cos(angle), np.sin(angle)], axis=1)
    to_lane = both[:128]
    to_row = both[:128].T
    from_row = both[:128]
    from_lane = both.T
    return tuple(t.astype(ml_dtypes.bfloat16) for t in (to_lane, to_row, from_row, from_lane))


def dot(left, right):
    return jnp.dot(left, right, preferred_element_type=F32)


def spectrum_product(left, right):
    lcc, lcs, lsc, lss = left[:128, :128], left[:128, 128:], left[128:, :128], left[128:, 128:]
    rcc, rcs, rsc, rss = right[:128, :128], right[:128, 128:], right[128:, :128], right[128:, 128:]
    cc = lcc * rcc - lcs * rcs - lsc * rsc + lss * rss
    cs = lcc * rcs + lcs * rcc - lsc * rss - lss * rsc
    sc = lcc * rsc - lcs * rss + lsc * rcc - lss * rcs
    ss = lcc * rss + lcs * rsc + lsc * rcs + lss * rcc
    top = jnp.concatenate([cc, cs], axis=1)
    bottom = jnp.concatenate([sc, ss], axis=1)
    return jnp.concatenate([top, bottom], axis=0).astype(BF16)


def kernel(
    kv_ref, gate_ref, filt_ref, skip_ref, w_ref, to_lane, to_row, from_row, from_lane,
    out_ref,
    spread, send_a, recv_a, rows_x, rows_h, rows_y, send_c, recv_c, rows_c,
    gated, weights, acc, part_out, part_in,
    a_send, a_recv, c_send, c_recv, w1_send, w1_recv, w2_send, w2_recv, w3_send, w3_recv, w_local,
    right_send, right_recv, left_send, left_recv, y_send, y_recv,
):
    me = lax.axis_index("seq")
    chan = lax.axis_index("chan")
    y_hi = chan // Z
    z = lax.rem(chan, Z)
    core = lax.rem(me, 2)
    x = me // 8
    share = x * 2 + core

    def chan_of(hi, zz):
        return hi * Z + lax.rem(zz, Z)

    right, left = chan_of(y_hi, z + 1), chan_of(y_hi, z + Z - 1)
    partner = chan_of(1 - y_hi, z)
    barrier = pltpu.get_barrier_semaphore()

    def greet_seq(k, carry):
        pl.semaphore_signal(
            barrier, inc=1, device_id={"seq": lax.rem(me + k, SEQ)}, device_id_type=MESH
        )
        return carry

    def greet_z(k, carry):
        pl.semaphore_signal(
            barrier, inc=1, device_id={"chan": chan_of(y_hi, z + k)}, device_id_type=MESH
        )
        return carry

    lax.fori_loop(1, SEQ, greet_seq, 0)
    lax.fori_loop(1, Z, greet_z, 0)
    pl.semaphore_signal(barrier, inc=1, device_id={"chan": partner}, device_id_type=MESH)

    for which, source in enumerate((kv_ref, filt_ref)):
        for seg in range(SEGS):
            for part in range(CH // LANES):
                block = source[seg * LANES : (seg + 1) * LANES, part * LANES : (part + 1) * LANES]
                turned = block.astype(F32).T
                for quarter in range(LANES // SEQ):
                    index = part * (LANES // SEQ) + quarter
                    half, own = index // OWN, index % OWN
                    spread[half, pl.ds(seg * OWN + own, SEQ, stride=ROWS), :] = turned[
                        quarter * SEQ : (quarter + 1) * SEQ
                    ]
        for half in range(HALVES):
            send_a[half, :, which * ROWS : (which + 1) * ROWS, :] = (
                spread[half].reshape(SEQ, ROWS, LANES).astype(BF16)
            )
    for half in range(HALVES):
        recv_a[half, me] = send_a[half, me]

    own_copies = [
        pltpu.make_async_copy(
            w_ref.at[
                pl.ds(pl.multiple_of(share * SHARE, SHARE), SHARE),
                pl.ds(
                    pl.multiple_of((y_hi + rel - 2 * y_hi * rel) * Z * CH + z * CH, CH), CH
                ),
            ],
            weights.at[share, z, rel],
            w_local.at[rel],
        )
        for rel in range(2)
    ]
    for copy in own_copies:
        copy.start()

    pl.semaphore_wait(barrier, SEQ - 1 + Z - 1 + 1)

    def send_signal(half):
        def one(k, carry):
            peer = lax.rem(me + k, SEQ)
            pltpu.make_async_remote_copy(
                src_ref=send_a.at[half, peer],
                dst_ref=recv_a.at[half, me],
                send_sem=a_send.at[half],
                recv_sem=a_recv.at[half],
                device_id={"seq": peer},
                device_id_type=MESH,
            ).start()
            return carry

        lax.fori_loop(1, SEQ, one, 0)

    def wait_bytes(ref, sem):
        pltpu.make_async_copy(ref, ref, sem).wait()

    for half in range(HALVES):
        send_signal(half)

    def send_weight(k, carry):
        to = lax.rem(z + k, Z)
        for rel in range(2):
            column = (y_hi + rel - 2 * y_hi * rel) * Z * CH + to * CH
            pltpu.make_async_remote_copy(
                src_ref=w_ref.at[
                    pl.ds(pl.multiple_of(share * SHARE, SHARE), SHARE),
                    pl.ds(pl.multiple_of(column, CH), CH),
                ],
                dst_ref=weights.at[share, z, rel],
                send_sem=w1_send,
                recv_sem=w1_recv,
                device_id={"chan": chan_of(y_hi, to)},
                device_id_type=MESH,
            ).start()
        return carry

    lax.fori_loop(1, Z, send_weight, 0)

    def convolve(half):
        rows_x[...] = recv_a[half, :, :ROWS, :].astype(F32).reshape(SEQ * ROWS, LANES)
        rows_h[...] = recv_a[half, :, ROWS:, :].astype(F32).reshape(SEQ * ROWS, LANES)
        first_row = lax.broadcasted_iota(jnp.int32, (LANES, LANES), 0) == 0
        for own in range(OWN):
            spectra = []
            for rows in (rows_x, rows_h):
                blocks = rows[pl.ds(own, LANES, stride=OWN), :].astype(BF16)
                lane_freq = dot(blocks, to_lane[...]).astype(BF16)
                spectra.append(dot(to_row[...], lane_freq))
            product = spectrum_product(*spectra)
            back = dot(from_row[...], product).astype(BF16)
            wide = dot(back, from_lane[...])
            carried = jnp.where(first_row, 0.0, pltpu.roll(wide[:, LANES:], 1, 0))
            rows_y[pl.ds(own, LANES, stride=OWN), :] = (wide[:, :LANES] + carried) * (
                1.0 / (128 * 128)
            )
        send_c[half] = rows_y[...].reshape(SEQ, ROWS, LANES).astype(BF16)
        recv_c[half, me] = send_c[half, me]

    def send_back(half):
        def one(k, carry):
            peer = lax.rem(me + k, SEQ)
            pltpu.make_async_remote_copy(
                src_ref=send_c.at[half, peer],
                dst_ref=recv_c.at[half, me],
                send_sem=c_send.at[half],
                recv_sem=c_recv.at[half],
                device_id={"seq": peer},
                device_id_type=MESH,
            ).start()
            return carry

        lax.fori_loop(1, SEQ, one, 0)

    others = pl.ds(0, SEQ - 1)

    def second_leg(k, carry):
        peer = lax.rem(me + 8 * k, SEQ)
        pltpu.make_async_remote_copy(
            src_ref=weights.at[share],
            dst_ref=weights.at[share],
            send_sem=w2_send,
            recv_sem=w2_recv,
            device_id={"seq": peer},
            device_id_type=MESH,
        ).start()
        return carry

    def third_leg(k, carry):
        which = 2 * k + core
        pltpu.make_async_remote_copy(
            src_ref=weights.at[which],
            dst_ref=weights.at[which],
            send_sem=w3_send,
            recv_sem=w3_recv,
            device_id={"seq": me + 1 - 2 * core},
            device_id_type=MESH,
        ).start()
        return carry

    seven = weights.at[0, pl.ds(0, Z - 1)]
    for half in range(HALVES):
        wait_bytes(recv_a.at[half, others], a_recv.at[half])
        convolve(half)
        send_back(half)
        if half == 0:
            for copy in own_copies:
                copy.wait()
            wait_bytes(seven, w1_recv)
            lax.fori_loop(1, 4, second_leg, 0)
    wait_bytes(weights.at[pl.ds(0, 3)], w2_recv)
    lax.fori_loop(0, 4, third_leg, 0)

    def piece(block, half, chunk):
        return gated.at[block, half, pl.ds(chunk * PIECE, PIECE)]

    def to_right(half, step, chunk):
        ref = piece(lax.rem(z - step + Z, Z), half, chunk)
        return pltpu.make_async_remote_copy(
            src_ref=ref,
            dst_ref=ref,
            send_sem=right_send.at[half, step, chunk],
            recv_sem=right_recv.at[half, step, chunk],
            device_id={"chan": right},
            device_id_type=MESH,
        )

    def to_left(half, step, chunk):
        ref = piece(lax.rem(z + step, Z), half, chunk)
        return pltpu.make_async_remote_copy(
            src_ref=ref,
            dst_ref=ref,
            send_sem=left_send.at[half, step, chunk],
            recv_sem=left_recv.at[half, step, chunk],
            device_id={"chan": left},
            device_id_type=MESH,
        )

    def arrive(ref, sem):
        pltpu.make_async_copy(ref, ref, sem).wait()

    def goes_right(step, chunk):
        return step < 3 or (step == 3 and chunk < TOK_CHUNKS // 2)

    def goes_left(step, chunk):
        return step < 3 or (step == 3 and chunk >= TOK_CHUNKS // 2)

    def add_block(block, half, first):
        shares = CHUNK_CH // SHARE
        for rel in range(2):
            weight = weights[half * shares : (half + 1) * shares, block, rel].reshape(CHUNK_CH, CH)
            term = dot(gated[block, half], weight)
            if first:
                acc[rel] = term
            else:
                acc[rel] += term

    for half in range(HALVES):
        wait_bytes(recv_c.at[half, others], c_recv.at[half])
        rows_c[...] = recv_c[half].astype(F32).reshape(SEQ * ROWS, LANES)
        for seg in range(SEGS):
            columns = []
            for part in range(CHUNK_CH // LANES):
                per = LANES // SEQ
                stacked = jnp.concatenate(
                    [
                        rows_c[pl.ds(seg * OWN + part * per + own, SEQ, stride=ROWS), :]
                        for own in range(per)
                    ],
                    axis=0,
                )
                columns.append(stacked.T)
            conv = jnp.concatenate(columns, axis=1) if len(columns) > 1 else columns[0]
            tokens = slice(seg * LANES, (seg + 1) * LANES)
            chans = slice(half * CHUNK_CH, (half + 1) * CHUNK_CH)
            signal = kv_ref[tokens, chans].astype(F32)
            value = gate_ref[tokens, chans].astype(F32) * (conv + skip_ref[:, chans] * signal)
            gated[z, half, tokens, :] = value.astype(BF16)
        for chunk in range(TOK_CHUNKS):
            to_right(half, 0, chunk).start()
            to_left(half, 0, chunk).start()

    wait_bytes(weights.at[pl.ds(0, 4)], w3_recv)

    for half in range(HALVES):
        add_block(z, half, half == 0)
        for step in range(4):
            from_left = lax.rem(z + Z - step - 1, Z)
            from_right = lax.rem(z + step + 1, Z)
            for chunk in range(TOK_CHUNKS):
                if goes_right(step, chunk):
                    arrive(piece(from_left, half, chunk), right_recv.at[half, step, chunk])
                    if goes_right(step + 1, chunk):
                        to_right(half, step + 1, chunk).start()
                if goes_left(step, chunk):
                    arrive(piece(from_right, half, chunk), left_recv.at[half, step, chunk])
                    if goes_left(step + 1, chunk):
                        to_left(half, step + 1, chunk).start()
            add_block(from_left, half, False)
            if step < 3:
                add_block(from_right, half, False)

    part_out[...] = acc[1].astype(BF16)
    exchange = pltpu.make_async_remote_copy(
        src_ref=part_out,
        dst_ref=part_in,
        send_sem=y_send,
        recv_sem=y_recv,
        device_id={"chan": partner},
        device_id_type=MESH,
    )
    exchange.start()

    for half in range(HALVES):
        wait_bytes(send_a.at[half, others], a_send.at[half])
        wait_bytes(send_c.at[half, others], c_send.at[half])
        for step in range(4):
            for chunk in range(TOK_CHUNKS):
                if goes_right(step, chunk):
                    arrive(piece(0, half, chunk), right_send.at[half, step, chunk])
                if goes_left(step, chunk):
                    arrive(piece(0, half, chunk), left_send.at[half, step, chunk])
    wait_bytes(seven, w1_send)
    wait_bytes(weights.at[pl.ds(0, 3)], w2_send)
    wait_bytes(weights.at[pl.ds(0, 4)], w3_send)
    exchange.wait()
    out_ref[...] = (acc[0] + part_in[...].astype(F32)).astype(BF16)


def per_device(key_value, gating, long_filter, skip_gain, out_weight):
    vmem = pl.BlockSpec(memory_space=pltpu.VMEM)
    anywhere = pl.BlockSpec(memory_space=pl.ANY)
    dma = pltpu.SemaphoreType.DMA
    ring = dma((HALVES, 4, TOK_CHUNKS))
    return pl.pallas_call(
        kernel,
        out_shape=jax.ShapeDtypeStruct((TOK, CH), BF16),
        in_specs=[vmem, vmem, vmem, vmem, anywhere, vmem, vmem, vmem, vmem],
        out_specs=vmem,
        scratch_shapes=[
            pltpu.VMEM((HALVES, SEQ * ROWS, LANES), F32),
            pltpu.VMEM((HALVES, SEQ, 2 * ROWS, LANES), BF16),
            pltpu.VMEM((HALVES, SEQ, 2 * ROWS, LANES), BF16),
            pltpu.VMEM((SEQ * ROWS, LANES), F32),
            pltpu.VMEM((SEQ * ROWS, LANES), F32),
            pltpu.VMEM((SEQ * ROWS, LANES), F32),
            pltpu.VMEM((HALVES, SEQ, ROWS, LANES), BF16),
            pltpu.VMEM((HALVES, SEQ, ROWS, LANES), BF16),
            pltpu.VMEM((SEQ * ROWS, LANES), F32),
            pltpu.VMEM((Z, HALVES, TOK, CHUNK_CH), BF16),
            pltpu.VMEM((SHARES, Z, 2, SHARE, CH), BF16),
            pltpu.VMEM((2, TOK, CH), F32),
            pltpu.VMEM((TOK, CH), BF16),
            pltpu.VMEM((TOK, CH), BF16),
            dma((HALVES,)), dma((HALVES,)), dma((HALVES,)), dma((HALVES,)),
            dma, dma, dma, dma, dma, dma, dma((2,)),
            ring, ring, ring, ring,
            dma, dma,
        ],
        compiler_params=pltpu.CompilerParams(
            collective_id=0, has_side_effects=True, vmem_limit_bytes=48 * 2**20
        ),
    )(
        key_value, gating, long_filter, skip_gain.reshape(1, CH), out_weight,
        *(jnp.asarray(t) for t in tables()),
    )


def solution(mesh):
    return jax.shard_map(
        per_device,
        mesh=mesh,
        in_specs=(P("seq", "chan"), P("seq", "chan"), P("seq", "chan"), P("chan"), P("chan", None)),
        out_specs=P("seq", "chan"),
        check_vma=False,
    )
```

```python
import functools

import jax
import jax.numpy as jnp
import ml_dtypes
import numpy as np
from jax import lax
from jax.experimental import pallas as pl
from jax.experimental.pallas import tpu as pltpu
from jax.sharding import PartitionSpec as P

MESH = pl.DeviceIdType.MESH
F32 = jnp.float32
BF16 = jnp.bfloat16
SEQ = 32
Z = 8
LANES = 128
TOK = 512
CH = 256
SEGS = TOK // LANES
HALVES = 2
CHUNK_CH = CH // HALVES
OWN = CHUNK_CH // SEQ
ROWS = OWN * SEGS
TOK_CHUNKS = 4
PIECE = TOK // TOK_CHUNKS
GROUPS = 2
GROUP = TOK // GROUPS
ORDER = (
    (0, 0, 1), (0, 1, 1), (1, 0, 0), (0, 0, 2), (0, 1, 2), (1, 0, 1), (1, 1, -1), (0, 0, 3), (0, 1, 3),
    (1, 0, 2), (1, 1, 0), (1, 0, 3), (1, 1, 1), (1, 1, 2), (1, 1, 3),
)
SHARE = 32
SHARES = CH // SHARE


def tables():
    freq = (2 * np.arange(128) + 1) * np.pi / 256
    angle = np.arange(256)[:, None] * freq[None, :]
    both = np.concatenate([np.cos(angle), np.sin(angle)], axis=1)
    to_lane = both[:128]
    to_row = both[:128].T
    from_row = both[:128]
    from_lane = both.T
    return tuple(t.astype(ml_dtypes.bfloat16) for t in (to_lane, to_row, from_row, from_lane))


def dot(left, right):
    return jnp.dot(left, right, preferred_element_type=F32)


def spectrum_product(left, right):
    lcc, lcs, lsc, lss = left[:128, :128], left[:128, 128:], left[128:, :128], left[128:, 128:]
    rcc, rcs, rsc, rss = right[:128, :128], right[:128, 128:], right[128:, :128], right[128:, 128:]
    cc = lcc * rcc - lcs * rcs - lsc * rsc + lss * rss
    cs = lcc * rcs + lcs * rcc - lsc * rss - lss * rsc
    sc = lcc * rsc - lcs * rss + lsc * rcc - lss * rcs
    ss = lcc * rss + lcs * rsc + lsc * rcs + lss * rcc
    top = jnp.concatenate([cc, cs], axis=1)
    bottom = jnp.concatenate([sc, ss], axis=1)
    return jnp.concatenate([top, bottom], axis=0).astype(BF16)


def kernel(
    kv_hbm, gate_hbm, filt_hbm, skip_hbm, w_ref, to_lane_hbm, to_row_hbm, from_row_hbm, from_lane_hbm,
    out_ref,
    kv_ref, gate_ref, filt_ref, skip_ref, to_lane, to_row, from_row, from_lane, load_sem,
    spread, send_a, recv_a, rows_x, rows_h, rows_y, send_c, recv_c, rows_c,
    gated, weights, acc, part_out, part_in,
    a_send, a_recv, c_send, c_recv, w1_send, w1_recv, w2_send, w2_recv, w3_send, w3_recv, w_local,
    right_send, right_recv, left_send, left_recv, y_send, y_recv,
):
    me = lax.axis_index("seq")
    chan = lax.axis_index("chan")
    y_hi = chan // Z
    z = lax.rem(chan, Z)
    core = lax.rem(me, 2)
    x = me // 8
    share = x * 2 + core

    def chan_of(hi, zz):
        return hi * Z + lax.rem(zz, Z)

    right, left = chan_of(y_hi, z + 1), chan_of(y_hi, z + Z - 1)
    partner = chan_of(1 - y_hi, z)
    barrier = pltpu.get_barrier_semaphore()

    def greet_seq(k, carry):
        pl.semaphore_signal(
            barrier, inc=1, device_id={"seq": lax.rem(me + k, SEQ)}, device_id_type=MESH
        )
        return carry

    def greet_z(k, carry):
        pl.semaphore_signal(
            barrier, inc=1, device_id={"chan": chan_of(y_hi, z + k)}, device_id_type=MESH
        )
        return carry

    lax.fori_loop(1, SEQ, greet_seq, 0)
    lax.fori_loop(1, Z, greet_z, 0)
    pl.semaphore_signal(barrier, inc=1, device_id={"chan": partner}, device_id_type=MESH)

    loads = [
        pltpu.make_async_copy(source, target, load_sem.at[at])
        for at, (source, target) in enumerate(
            (
                (kv_hbm, kv_ref), (filt_hbm, filt_ref), (to_lane_hbm, to_lane), (to_row_hbm, to_row),
                (from_row_hbm, from_row), (from_lane_hbm, from_lane), (gate_hbm, gate_ref), (skip_hbm, skip_ref),
            )
        )
    ]
    for load in loads:
        load.start()
    loads[0].wait()
    loads[1].wait()

    for which, source in enumerate((kv_ref, filt_ref)):
        for seg in range(SEGS):
            for part in range(CH // LANES):
                block = source[seg * LANES : (seg + 1) * LANES, part * LANES : (part + 1) * LANES]
                turned = block.astype(F32).T
                for quarter in range(LANES // SEQ):
                    index = part * (LANES // SEQ) + quarter
                    half, own = index // OWN, index % OWN
                    spread[half, pl.ds(seg * OWN + own, SEQ, stride=ROWS), :] = turned[
                        quarter * SEQ : (quarter + 1) * SEQ
                    ]
        for half in range(HALVES):
            send_a[half, :, which * ROWS : (which + 1) * ROWS, :] = (
                spread[half].reshape(SEQ, ROWS, LANES).astype(BF16)
            )
    for half in range(HALVES):
        recv_a[half, me] = send_a[half, me]

    own_copies = [
        pltpu.make_async_copy(
            w_ref.at[
                pl.ds(pl.multiple_of(share * SHARE, SHARE), SHARE),
                pl.ds(
                    pl.multiple_of((y_hi + rel - 2 * y_hi * rel) * Z * CH + z * CH, CH), CH
                ),
            ],
            weights.at[share, z, rel],
            w_local.at[rel],
        )
        for rel in range(2)
    ]
    for copy in own_copies:
        copy.start()

    for load in loads[2:]:
        load.wait()
    for copy in own_copies:
        copy.wait()
    pl.semaphore_wait(barrier, SEQ - 1 + Z - 1 + 1)

    def send_signal(half):
        def one(k, carry):
            peer = lax.rem(me + k, SEQ)
            pltpu.make_async_remote_copy(
                src_ref=send_a.at[half, peer],
                dst_ref=recv_a.at[half, me],
                send_sem=a_send.at[half],
                recv_sem=a_recv.at[half],
                device_id={"seq": peer},
                device_id_type=MESH,
            ).start()
            return carry

        lax.fori_loop(1, SEQ, one, 0)

    def wait_bytes(ref, sem):
        pltpu.make_async_copy(ref, ref, sem).wait()

    def send_weight(k, carry):
        to = lax.rem(z + k, Z)
        for rel in range(2):
            column = (y_hi + rel - 2 * y_hi * rel) * Z * CH + to * CH
            pltpu.make_async_remote_copy(
                src_ref=w_ref.at[
                    pl.ds(pl.multiple_of(share * SHARE, SHARE), SHARE),
                    pl.ds(pl.multiple_of(column, CH), CH),
                ],
                dst_ref=weights.at[share, z, rel],
                send_sem=w1_send,
                recv_sem=w1_recv,
                device_id={"chan": chan_of(y_hi, to)},
                device_id_type=MESH,
            ).start()
        return carry

    lax.fori_loop(1, Z, send_weight, 0)
    for half in range(HALVES):
        send_signal(half)

    def convolve(half):
        rows_x[...] = recv_a[half, :, :ROWS, :].astype(F32).reshape(SEQ * ROWS, LANES)
        rows_h[...] = recv_a[half, :, ROWS:, :].astype(F32).reshape(SEQ * ROWS, LANES)
        first_row = lax.broadcasted_iota(jnp.int32, (LANES, LANES), 0) == 0
        for own in range(OWN):
            spectra = []
            for rows in (rows_x, rows_h):
                blocks = rows[pl.ds(own, LANES, stride=OWN), :].astype(BF16)
                lane_freq = dot(blocks, to_lane[...]).astype(BF16)
                spectra.append(dot(to_row[...], lane_freq))
            product = spectrum_product(*spectra)
            back = dot(from_row[...], product).astype(BF16)
            wide = dot(back, from_lane[...])
            carried = jnp.where(first_row, 0.0, pltpu.roll(wide[:, LANES:], 1, 0))
            rows_y[pl.ds(own, LANES, stride=OWN), :] = (wide[:, :LANES] + carried) * (
                1.0 / (128 * 128)
            )
        send_c[half] = rows_y[...].reshape(SEQ, ROWS, LANES).astype(BF16)
        recv_c[half, me] = send_c[half, me]

    def send_back(half):
        def one(k, carry):
            peer = lax.rem(me + k, SEQ)
            pltpu.make_async_remote_copy(
                src_ref=send_c.at[half, peer],
                dst_ref=recv_c.at[half, me],
                send_sem=c_send.at[half],
                recv_sem=c_recv.at[half],
                device_id={"seq": peer},
                device_id_type=MESH,
            ).start()
            return carry

        lax.fori_loop(1, SEQ, one, 0)

    others = pl.ds(0, SEQ - 1)

    def second_leg(k, carry):
        peer = lax.rem(me + 8 * k, SEQ)
        pltpu.make_async_remote_copy(
            src_ref=weights.at[share],
            dst_ref=weights.at[share],
            send_sem=w2_send,
            recv_sem=w2_recv,
            device_id={"seq": peer},
            device_id_type=MESH,
        ).start()
        return carry

    def third_leg(k, carry):
        which = 2 * k + core
        pltpu.make_async_remote_copy(
            src_ref=weights.at[which],
            dst_ref=weights.at[which],
            send_sem=w3_send,
            recv_sem=w3_recv,
            device_id={"seq": me + 1 - 2 * core},
            device_id_type=MESH,
        ).start()
        return carry

    seven = weights.at[0, pl.ds(0, Z - 1)]
    wait_bytes(seven, w1_recv)
    lax.fori_loop(1, 4, second_leg, 0)
    for half in range(HALVES):
        wait_bytes(recv_a.at[half, others], a_recv.at[half])
        convolve(half)
        send_back(half)

    def piece(block, half, chunk):
        return gated.at[block, half, pl.ds(chunk * PIECE, PIECE)]

    def to_right(half, step, chunk):
        ref = piece(lax.rem(z - step + Z, Z), half, chunk)
        return pltpu.make_async_remote_copy(
            src_ref=ref,
            dst_ref=ref,
            send_sem=right_send.at[half, step, chunk],
            recv_sem=right_recv.at[half, step, chunk],
            device_id={"chan": right},
            device_id_type=MESH,
        )

    def to_left(half, step, chunk):
        ref = piece(lax.rem(z + step, Z), half, chunk)
        return pltpu.make_async_remote_copy(
            src_ref=ref,
            dst_ref=ref,
            send_sem=left_send.at[half, step, chunk],
            recv_sem=left_recv.at[half, step, chunk],
            device_id={"chan": left},
            device_id_type=MESH,
        )

    def arrive(ref, sem):
        pltpu.make_async_copy(ref, ref, sem).wait()

    def goes_right(step, chunk):
        return step < 3 or (step == 3 and chunk % 2 == 0)

    def goes_left(step, chunk):
        return step < 3 or (step == 3 and chunk % 2 == 1)

    def tokens_of(group):
        return pl.ds(group * GROUP, GROUP)

    def chunks_of(group):
        per = TOK_CHUNKS // GROUPS
        return range(group * per, (group + 1) * per)

    def add_block(block, half, group, first=False):
        shares = CHUNK_CH // SHARE
        tokens = tokens_of(group)
        for rel in range(2):
            weight = weights[half * shares : (half + 1) * shares, block, rel].reshape(CHUNK_CH, CH)
            term = dot(gated[block, half, tokens], weight)
            if first:
                acc[rel, tokens] = term
            else:
                acc[rel, tokens] += term

    def gate(half):
        wait_bytes(recv_c.at[half, others], c_recv.at[half])
        rows_c[...] = recv_c[half].astype(F32).reshape(SEQ * ROWS, LANES)
        for seg in range(SEGS):
            columns = []
            for part in range(CHUNK_CH // LANES):
                per = LANES // SEQ
                stacked = jnp.concatenate(
                    [
                        rows_c[pl.ds(seg * OWN + part * per + own, SEQ, stride=ROWS), :]
                        for own in range(per)
                    ],
                    axis=0,
                )
                columns.append(stacked.T)
            conv = jnp.concatenate(columns, axis=1) if len(columns) > 1 else columns[0]
            tokens = slice(seg * LANES, (seg + 1) * LANES)
            chans = slice(half * CHUNK_CH, (half + 1) * CHUNK_CH)
            signal = kv_ref[tokens, chans].astype(F32)
            value = gate_ref[tokens, chans].astype(F32) * (conv + skip_ref[:, chans] * signal)
            gated[z, half, tokens, :] = value.astype(BF16)

    def start_group(half, group):
        for chunk in chunks_of(group):
            to_right(half, 0, chunk).start()
            to_left(half, 0, chunk).start()

    def sources(step):
        return lax.rem(z + Z - step - 1, Z), lax.rem(z + step + 1, Z)

    def pass_on(half, group, step):
        from_left, from_right = sources(step)
        for chunk in chunks_of(group):
            if goes_right(step, chunk):
                arrive(piece(from_left, half, chunk), right_recv.at[half, step, chunk])
                if goes_right(step + 1, chunk):
                    to_right(half, step + 1, chunk).start()
            if goes_left(step, chunk):
                arrive(piece(from_right, half, chunk), left_recv.at[half, step, chunk])
                if goes_left(step + 1, chunk):
                    to_left(half, step + 1, chunk).start()

    def add_step(half, group, step):
        from_left, from_right = sources(step)
        add_block(from_left, half, group)
        if step < 3:
            add_block(from_right, half, group)

    gate(0)
    for group in range(GROUPS):
        start_group(0, group)
    wait_bytes(weights.at[pl.ds(0, 3)], w2_recv)
    lax.fori_loop(0, 4, third_leg, 0)
    for group in range(GROUPS):
        pass_on(0, group, 0)
    gate(1)
    start_group(1, 0)
    wait_bytes(weights.at[pl.ds(0, 4)], w3_recv)
    for group in range(GROUPS):
        add_block(z, 0, group, True)
        add_block(z, 1, group)
        add_step(0, group, 0)

    exchanges = []
    for half, group, step in ORDER:
        if step < 0:
            start_group(half, group)
            continue
        pass_on(half, group, step)
        add_step(half, group, step)
        if half == HALVES - 1 and step == 3:
            tokens = tokens_of(group)
            part_out[tokens] = acc[1, tokens].astype(BF16)
            exchange = pltpu.make_async_remote_copy(
                src_ref=part_out.at[tokens],
                dst_ref=part_in.at[tokens],
                send_sem=y_send.at[group],
                recv_sem=y_recv.at[group],
                device_id={"chan": partner},
                device_id_type=MESH,
            )
            exchange.start()
            exchanges.append((group, exchange))

    for half in range(HALVES):
        wait_bytes(send_a.at[half, others], a_send.at[half])
        wait_bytes(send_c.at[half, others], c_send.at[half])
        for step in range(4):
            for chunk in range(TOK_CHUNKS):
                if goes_right(step, chunk):
                    arrive(piece(0, half, chunk), right_send.at[half, step, chunk])
                if goes_left(step, chunk):
                    arrive(piece(0, half, chunk), left_send.at[half, step, chunk])
    wait_bytes(seven, w1_send)
    wait_bytes(weights.at[pl.ds(0, 3)], w2_send)
    wait_bytes(weights.at[pl.ds(0, 4)], w3_send)
    for group, exchange in exchanges:
        tokens = tokens_of(group)
        exchange.wait()
        out_ref[tokens] = (acc[0, tokens] + part_in[tokens].astype(F32)).astype(BF16)


def per_device(key_value, gating, long_filter, skip_gain, out_weight):
    vmem = pl.BlockSpec(memory_space=pltpu.VMEM)
    anywhere = pl.BlockSpec(memory_space=pl.ANY)
    dma = pltpu.SemaphoreType.DMA
    ring = dma((HALVES, 4, TOK_CHUNKS))
    return pl.pallas_call(
        kernel,
        out_shape=jax.ShapeDtypeStruct((TOK, CH), BF16),
        in_specs=[anywhere] * 9,
        out_specs=vmem,
        scratch_shapes=[
            pltpu.VMEM((TOK, CH), BF16),
            pltpu.VMEM((TOK, CH), BF16),
            pltpu.VMEM((TOK, CH), BF16),
            pltpu.VMEM((1, CH), F32),
            pltpu.VMEM((128, 256), BF16),
            pltpu.VMEM((256, 128), BF16),
            pltpu.VMEM((128, 256), BF16),
            pltpu.VMEM((256, 256), BF16),
            dma((8,)),
            pltpu.VMEM((HALVES, SEQ * ROWS, LANES), F32),
            pltpu.VMEM((HALVES, SEQ, 2 * ROWS, LANES), BF16),
            pltpu.VMEM((HALVES, SEQ, 2 * ROWS, LANES), BF16),
            pltpu.VMEM((SEQ * ROWS, LANES), F32),
            pltpu.VMEM((SEQ * ROWS, LANES), F32),
            pltpu.VMEM((SEQ * ROWS, LANES), F32),
            pltpu.VMEM((HALVES, SEQ, ROWS, LANES), BF16),
            pltpu.VMEM((HALVES, SEQ, ROWS, LANES), BF16),
            pltpu.VMEM((SEQ * ROWS, LANES), F32),
            pltpu.VMEM((Z, HALVES, TOK, CHUNK_CH), BF16),
            pltpu.VMEM((SHARES, Z, 2, SHARE, CH), BF16),
            pltpu.VMEM((2, TOK, CH), F32),
            pltpu.VMEM((TOK, CH), BF16),
            pltpu.VMEM((TOK, CH), BF16),
            dma((HALVES,)), dma((HALVES,)), dma((HALVES,)), dma((HALVES,)),
            dma, dma, dma, dma, dma, dma, dma((2,)),
            ring, ring, ring, ring,
            dma((GROUPS,)), dma((GROUPS,)),
        ],
        compiler_params=pltpu.CompilerParams(
            collective_id=0, has_side_effects=True, vmem_limit_bytes=60 * 2**20
        ),
    )(
        key_value, gating, long_filter, skip_gain.reshape(1, CH), out_weight,
        *(jnp.asarray(t) for t in tables()),
    )


def solution(mesh):
    return jax.shard_map(
        per_device,
        mesh=mesh,
        in_specs=(P("seq", "chan"), P("seq", "chan"), P("seq", "chan"), P("chan"), P("chan", None)),
        out_specs=P("seq", "chan"),
        check_vma=False,
    )
```

```python
import functools

import jax
import jax.numpy as jnp
import ml_dtypes
import numpy as np
from jax import lax
from jax.experimental import pallas as pl
from jax.experimental.pallas import tpu as pltpu
from jax.sharding import PartitionSpec as P

MESH = pl.DeviceIdType.MESH
F32 = jnp.float32
BF16 = jnp.bfloat16
SEQ = 32
Z = 8
LANES = 128
TOK = 512
CH = 256
SEGS = TOK // LANES
HALVES = 2
CHUNK_CH = CH // HALVES
OWN = CHUNK_CH // SEQ
ROWS = OWN * SEGS
TOK_CHUNKS = 4
PIECE = TOK // TOK_CHUNKS
GROUPS = 2
GROUP = TOK // GROUPS
ORDER = (
    ("conv", 0), ("gate", 0), ("start", 0, 0), ("start", 0, 1), ("conv", 1), ("step", 0, 0, 0), ("step", 0, 1, 0),
    ("legs",), ("gate", 1), ("start", 1, 0), ("step", 0, 0, 1), ("step", 0, 1, 1), ("weights",), ("start", 1, 1),
    ("step", 1, 0, 0), ("step", 0, 0, 2), ("step", 0, 1, 2), ("step", 1, 0, 1), ("step", 1, 1, 0), ("step", 0, 0, 3),
    ("step", 0, 1, 3), ("step", 1, 0, 2), ("step", 1, 1, 1), ("step", 1, 0, 3), ("step", 1, 1, 2), ("step", 1, 1, 3),
)
SHARES = (8, 2)
SERIAL = True


def tables():
    freq = (2 * np.arange(128) + 1) * np.pi / 256
    angle = np.arange(256)[:, None] * freq[None, :]
    both = np.concatenate([np.cos(angle), np.sin(angle)], axis=1)
    to_lane = both[:128]
    to_row = both[:128].T
    from_row = both[:128]
    from_lane = both.T
    return tuple(t.astype(ml_dtypes.bfloat16) for t in (to_lane, to_row, from_row, from_lane))


def dot(left, right):
    return jnp.dot(left, right, preferred_element_type=F32)


def spectrum_product(left, right):
    lcc, lcs, lsc, lss = left[:128, :128], left[:128, 128:], left[128:, :128], left[128:, 128:]
    rcc, rcs, rsc, rss = right[:128, :128], right[:128, 128:], right[128:, :128], right[128:, 128:]
    cc = lcc * rcc - lcs * rcs - lsc * rsc + lss * rss
    cs = lcc * rcs + lcs * rcc - lsc * rss - lss * rsc
    sc = lcc * rsc - lcs * rss + lsc * rcc - lss * rcs
    ss = lcc * rss + lcs * rsc + lsc * rcs + lss * rcc
    top = jnp.concatenate([cc, cs], axis=1)
    bottom = jnp.concatenate([sc, ss], axis=1)
    return jnp.concatenate([top, bottom], axis=0).astype(BF16)


def kernel(
    kv_hbm, gate_hbm, filt_hbm, skip_hbm, w_ref, to_lane_hbm, to_row_hbm, from_row_hbm, from_lane_hbm,
    out_ref,
    kv_ref, gate_ref, filt_ref, skip_ref, to_lane, to_row, from_row, from_lane, load_sem,
    spread, send_a, recv_a, rows_x, rows_h, rows_y, send_c, recv_c, rows_c,
    gated, weights_0, weights_1, acc, part_out, part_in,
    a_send, a_recv, c_send, c_recv, w1_send, w1_recv, w2_send, w2_recv, w3_send, w3_recv, w_local,
    right_send, right_recv, left_send, left_recv, y_send, y_recv,
):
    me = lax.axis_index("seq")
    chan = lax.axis_index("chan")
    y_hi = chan // Z
    z = lax.rem(chan, Z)
    core = lax.rem(me, 2)
    x = me // 8
    shares = [x * 2 + core if SHARES[half] == 8 else core for half in range(HALVES)]
    weights = (weights_0, weights_1)
    depths = [CHUNK_CH // SHARES[half] for half in range(HALVES)]

    def weight_piece(half, to, rel):
        row = half * CHUNK_CH + shares[half] * depths[half]
        column = (y_hi + rel - 2 * y_hi * rel) * Z * CH + to * CH
        return w_ref.at[
            pl.ds(pl.multiple_of(row, depths[half]), depths[half]), pl.ds(pl.multiple_of(column, CH), CH)
        ]


    def chan_of(hi, zz):
        return hi * Z + lax.rem(zz, Z)

    right, left = chan_of(y_hi, z + 1), chan_of(y_hi, z + Z - 1)
    partner = chan_of(1 - y_hi, z)
    barrier = pltpu.get_barrier_semaphore()

    def greet_seq(k, carry):
        pl.semaphore_signal(
            barrier, inc=1, device_id={"seq": lax.rem(me + k, SEQ)}, device_id_type=MESH
        )
        return carry

    def greet_z(k, carry):
        pl.semaphore_signal(
            barrier, inc=1, device_id={"chan": chan_of(y_hi, z + k)}, device_id_type=MESH
        )
        return carry

    lax.fori_loop(1, SEQ, greet_seq, 0)
    lax.fori_loop(1, Z, greet_z, 0)
    pl.semaphore_signal(barrier, inc=1, device_id={"chan": partner}, device_id_type=MESH)

    loads = [
        pltpu.make_async_copy(source, target, load_sem.at[at])
        for at, (source, target) in enumerate(
            (
                (kv_hbm, kv_ref), (filt_hbm, filt_ref), (to_lane_hbm, to_lane), (to_row_hbm, to_row),
                (from_row_hbm, from_row), (from_lane_hbm, from_lane), (gate_hbm, gate_ref), (skip_hbm, skip_ref),
            )
        )
    ]
    for load in loads:
        load.start()
    loads[0].wait()
    loads[1].wait()

    for which, source in enumerate((kv_ref, filt_ref)):
        for seg in range(SEGS):
            for part in range(CH // LANES):
                block = source[seg * LANES : (seg + 1) * LANES, part * LANES : (part + 1) * LANES]
                turned = block.astype(F32).T
                for quarter in range(LANES // SEQ):
                    index = part * (LANES // SEQ) + quarter
                    half, own = index // OWN, index % OWN
                    spread[half, pl.ds(seg * OWN + own, SEQ, stride=ROWS), :] = turned[
                        quarter * SEQ : (quarter + 1) * SEQ
                    ]
        for half in range(HALVES):
            send_a[half, :, which * ROWS : (which + 1) * ROWS, :] = (
                spread[half].reshape(SEQ, ROWS, LANES).astype(BF16)
            )
    for half in range(HALVES):
        recv_a[half, me] = send_a[half, me]

    own_copies = [
        pltpu.make_async_copy(
            weight_piece(half, z, rel), weights[half].at[shares[half], z, rel], w_local.at[half, rel]
        )
        for half in range(HALVES)
        for rel in range(2)
    ]
    for copy in own_copies:
        copy.start()

    for load in loads[2:]:
        load.wait()
    for copy in own_copies:
        copy.wait()
    pl.semaphore_wait(barrier, SEQ - 1 + Z - 1 + 1)

    def send_signal(half):
        def one(k, carry):
            peer = lax.rem(me + k, SEQ)
            pltpu.make_async_remote_copy(
                src_ref=send_a.at[half, peer],
                dst_ref=recv_a.at[half, me],
                send_sem=a_send.at[half],
                recv_sem=a_recv.at[half],
                device_id={"seq": peer},
                device_id_type=MESH,
            ).start()
            return carry

        lax.fori_loop(1, SEQ, one, 0)

    def wait_bytes(ref, sem):
        pltpu.make_async_copy(ref, ref, sem).wait()

    for half in range(HALVES):

        def send_weight(k, carry, half=half):
            to = lax.rem(z + k, Z)
            for rel in range(2):
                pltpu.make_async_remote_copy(
                    src_ref=weight_piece(half, to, rel),
                    dst_ref=weights[half].at[shares[half], z, rel],
                    send_sem=w1_send.at[half],
                    recv_sem=w1_recv.at[half],
                    device_id={"chan": chan_of(y_hi, to)},
                    device_id_type=MESH,
                ).start()
            return carry

        lax.fori_loop(1, Z, send_weight, 0)
    others = pl.ds(0, SEQ - 1)
    send_signal(0)
    if SERIAL:
        wait_bytes(send_a.at[0, others], a_send.at[0])
    send_signal(1)

    def convolve(half):
        rows_x[...] = recv_a[half, :, :ROWS, :].astype(F32).reshape(SEQ * ROWS, LANES)
        rows_h[...] = recv_a[half, :, ROWS:, :].astype(F32).reshape(SEQ * ROWS, LANES)
        first_row = lax.broadcasted_iota(jnp.int32, (LANES, LANES), 0) == 0
        for own in range(OWN):
            spectra = []
            for rows in (rows_x, rows_h):
                blocks = rows[pl.ds(own, LANES, stride=OWN), :].astype(BF16)
                lane_freq = dot(blocks, to_lane[...]).astype(BF16)
                spectra.append(dot(to_row[...], lane_freq))
            product = spectrum_product(*spectra)
            back = dot(from_row[...], product).astype(BF16)
            wide = dot(back, from_lane[...])
            carried = jnp.where(first_row, 0.0, pltpu.roll(wide[:, LANES:], 1, 0))
            rows_y[pl.ds(own, LANES, stride=OWN), :] = (wide[:, :LANES] + carried) * (
                1.0 / (128 * 128)
            )
        send_c[half] = rows_y[...].reshape(SEQ, ROWS, LANES).astype(BF16)
        recv_c[half, me] = send_c[half, me]

    def send_back(half):
        def one(k, carry):
            peer = lax.rem(me + k, SEQ)
            pltpu.make_async_remote_copy(
                src_ref=send_c.at[half, peer],
                dst_ref=recv_c.at[half, me],
                send_sem=c_send.at[half],
                recv_sem=c_recv.at[half],
                device_id={"seq": peer},
                device_id_type=MESH,
            ).start()
            return carry

        lax.fori_loop(1, SEQ, one, 0)

    def first_leg_bytes(half):
        return weights[half].at[0, pl.ds(0, Z - 1)]

    def second_leg(half):
        if SHARES[half] == 2:
            return
        share = shares[half]

        def one(k, carry):
            pltpu.make_async_remote_copy(
                src_ref=weights[half].at[share],
                dst_ref=weights[half].at[share],
                send_sem=w2_send.at[half],
                recv_sem=w2_recv.at[half],
                device_id={"seq": lax.rem(me + 8 * k, SEQ)},
                device_id_type=MESH,
            ).start()
            return carry

        wait_bytes(first_leg_bytes(half), w1_recv.at[half])
        lax.fori_loop(1, 4, one, 0)

    def third_leg(half):
        if SHARES[half] == 2:
            wait_bytes(first_leg_bytes(half), w1_recv.at[half])
        else:
            wait_bytes(weights[half].at[pl.ds(0, 3)], w2_recv.at[half])

        def one(k, carry):
            which = 2 * k + core
            pltpu.make_async_remote_copy(
                src_ref=weights[half].at[which],
                dst_ref=weights[half].at[which],
                send_sem=w3_send.at[half],
                recv_sem=w3_recv.at[half],
                device_id={"seq": me + 1 - 2 * core},
                device_id_type=MESH,
            ).start()
            return carry

        lax.fori_loop(0, SHARES[half] // 2, one, 0)

    def third_leg_bytes(half):
        return weights[half].at[pl.ds(0, SHARES[half] // 2)]

    for half in range(HALVES):
        second_leg(half)
    def transform(half):
        wait_bytes(recv_a.at[half, others], a_recv.at[half])
        convolve(half)
        send_back(half)

    def piece(block, half, chunk):
        return gated.at[block, half, pl.ds(chunk * PIECE, PIECE)]

    def to_right(half, step, chunk):
        ref = piece(lax.rem(z - step + Z, Z), half, chunk)
        return pltpu.make_async_remote_copy(
            src_ref=ref,
            dst_ref=ref,
            send_sem=right_send.at[half, step, chunk],
            recv_sem=right_recv.at[half, step, chunk],
            device_id={"chan": right},
            device_id_type=MESH,
        )

    def to_left(half, step, chunk):
        ref = piece(lax.rem(z + step, Z), half, chunk)
        return pltpu.make_async_remote_copy(
            src_ref=ref,
            dst_ref=ref,
            send_sem=left_send.at[half, step, chunk],
            recv_sem=left_recv.at[half, step, chunk],
            device_id={"chan": left},
            device_id_type=MESH,
        )

    def arrive(ref, sem):
        pltpu.make_async_copy(ref, ref, sem).wait()

    def goes_right(step, chunk):
        return step < 3 or (step == 3 and chunk % 2 == 0)

    def goes_left(step, chunk):
        return step < 3 or (step == 3 and chunk % 2 == 1)

    def tokens_of(group):
        return pl.ds(group * GROUP, GROUP)

    def chunks_of(group):
        per = TOK_CHUNKS // GROUPS
        return range(group * per, (group + 1) * per)

    def add_block(block, half, group, first=False):
        tokens = tokens_of(group)
        for rel in range(2):
            weight = weights[half][:, block, rel].reshape(CHUNK_CH, CH)
            term = dot(gated[block, half, tokens], weight)
            if first:
                acc[rel, tokens] = term
            else:
                acc[rel, tokens] += term

    def gate(half):
        wait_bytes(recv_c.at[half, others], c_recv.at[half])
        rows_c[...] = recv_c[half].astype(F32).reshape(SEQ * ROWS, LANES)
        for seg in range(SEGS):
            columns = []
            for part in range(CHUNK_CH // LANES):
                per = LANES // SEQ
                stacked = jnp.concatenate(
                    [
                        rows_c[pl.ds(seg * OWN + part * per + own, SEQ, stride=ROWS), :]
                        for own in range(per)
                    ],
                    axis=0,
                )
                columns.append(stacked.T)
            conv = jnp.concatenate(columns, axis=1) if len(columns) > 1 else columns[0]
            tokens = slice(seg * LANES, (seg + 1) * LANES)
            chans = slice(half * CHUNK_CH, (half + 1) * CHUNK_CH)
            signal = kv_ref[tokens, chans].astype(F32)
            value = gate_ref[tokens, chans].astype(F32) * (conv + skip_ref[:, chans] * signal)
            gated[z, half, tokens, :] = value.astype(BF16)

    def start_group(half, group):
        for chunk in chunks_of(group):
            to_right(half, 0, chunk).start()
            to_left(half, 0, chunk).start()

    def sources(step):
        return lax.rem(z + Z - step - 1, Z), lax.rem(z + step + 1, Z)

    def pass_on(half, group, step):
        from_left, from_right = sources(step)
        for chunk in chunks_of(group):
            if goes_right(step, chunk):
                arrive(piece(from_left, half, chunk), right_recv.at[half, step, chunk])
                if goes_right(step + 1, chunk):
                    to_right(half, step + 1, chunk).start()
            if goes_left(step, chunk):
                arrive(piece(from_right, half, chunk), left_recv.at[half, step, chunk])
                if goes_left(step + 1, chunk):
                    to_left(half, step + 1, chunk).start()

    def add_step(half, group, step):
        from_left, from_right = sources(step)
        add_block(from_left, half, group)
        if step < 3:
            add_block(from_right, half, group)

    exchanges = []
    waiting = []

    def finish(half, group, step):
        add_step(half, group, step)
        if half < HALVES - 1 or step < 3:
            return
        tokens = tokens_of(group)
        part_out[tokens] = acc[1, tokens].astype(BF16)
        exchange = pltpu.make_async_remote_copy(
            src_ref=part_out.at[tokens],
            dst_ref=part_in.at[tokens],
            send_sem=y_send.at[group],
            recv_sem=y_recv.at[group],
            device_id={"chan": partner},
            device_id_type=MESH,
        )
        exchange.start()
        exchanges.append((group, exchange))

    for kind, *event in ORDER:
        if kind == "conv":
            transform(*event)
        elif kind == "start":
            start_group(*event)
        elif kind == "legs":
            for half in range(HALVES):
                third_leg(half)
        elif kind == "gate":
            gate(*event)
        elif kind == "weights":
            for half in range(HALVES):
                wait_bytes(third_leg_bytes(half), w3_recv.at[half])
            for group in range(GROUPS):
                add_block(z, 0, group, True)
                add_block(z, 1, group)
            for arrived in waiting:
                finish(*arrived)
            waiting = None
        else:
            pass_on(*event)
            if waiting is None:
                finish(*event)
            else:
                waiting.append(event)

    for half in range(HALVES):
        if half > 0 or not SERIAL:
            wait_bytes(send_a.at[half, others], a_send.at[half])
        wait_bytes(send_c.at[half, others], c_send.at[half])
        for step in range(4):
            for chunk in range(TOK_CHUNKS):
                if goes_right(step, chunk):
                    arrive(piece(0, half, chunk), right_send.at[half, step, chunk])
                if goes_left(step, chunk):
                    arrive(piece(0, half, chunk), left_send.at[half, step, chunk])
    for half in range(HALVES):
        wait_bytes(first_leg_bytes(half), w1_send.at[half])
        if SHARES[half] == 8:
            wait_bytes(weights[half].at[pl.ds(0, 3)], w2_send.at[half])
        wait_bytes(third_leg_bytes(half), w3_send.at[half])
    for group, exchange in exchanges:
        tokens = tokens_of(group)
        exchange.wait()
        out_ref[tokens] = (acc[0, tokens] + part_in[tokens].astype(F32)).astype(BF16)


def per_device(key_value, gating, long_filter, skip_gain, out_weight):
    vmem = pl.BlockSpec(memory_space=pltpu.VMEM)
    anywhere = pl.BlockSpec(memory_space=pl.ANY)
    dma = pltpu.SemaphoreType.DMA
    ring = dma((HALVES, 4, TOK_CHUNKS))
    return pl.pallas_call(
        kernel,
        out_shape=jax.ShapeDtypeStruct((TOK, CH), BF16),
        in_specs=[anywhere] * 9,
        out_specs=vmem,
        scratch_shapes=[
            pltpu.VMEM((TOK, CH), BF16),
            pltpu.VMEM((TOK, CH), BF16),
            pltpu.VMEM((TOK, CH), BF16),
            pltpu.VMEM((1, CH), F32),
            pltpu.VMEM((128, 256), BF16),
            pltpu.VMEM((256, 128), BF16),
            pltpu.VMEM((128, 256), BF16),
            pltpu.VMEM((256, 256), BF16),
            dma((8,)),
            pltpu.VMEM((HALVES, SEQ * ROWS, LANES), F32),
            pltpu.VMEM((HALVES, SEQ, 2 * ROWS, LANES), BF16),
            pltpu.VMEM((HALVES, SEQ, 2 * ROWS, LANES), BF16),
            pltpu.VMEM((SEQ * ROWS, LANES), F32),
            pltpu.VMEM((SEQ * ROWS, LANES), F32),
            pltpu.VMEM((SEQ * ROWS, LANES), F32),
            pltpu.VMEM((HALVES, SEQ, ROWS, LANES), BF16),
            pltpu.VMEM((HALVES, SEQ, ROWS, LANES), BF16),
            pltpu.VMEM((SEQ * ROWS, LANES), F32),
            pltpu.VMEM((Z, HALVES, TOK, CHUNK_CH), BF16),
            *(pltpu.VMEM((count, Z, 2, CHUNK_CH // count, CH), BF16) for count in SHARES),
            pltpu.VMEM((2, TOK, CH), F32),
            pltpu.VMEM((TOK, CH), BF16),
            pltpu.VMEM((TOK, CH), BF16),
            dma((HALVES,)), dma((HALVES,)), dma((HALVES,)), dma((HALVES,)),
            *(dma((HALVES,)) for _ in range(6)), dma((HALVES, 2)),
            ring, ring, ring, ring,
            dma((GROUPS,)), dma((GROUPS,)),
        ],
        compiler_params=pltpu.CompilerParams(
            collective_id=0, has_side_effects=True, vmem_limit_bytes=60 * 2**20
        ),
    )(
        key_value, gating, long_filter, skip_gain.reshape(1, CH), out_weight,
        *(jnp.asarray(t) for t in tables()),
    )


def solution(mesh):
    return jax.shard_map(
        per_device,
        mesh=mesh,
        in_specs=(P("seq", "chan"), P("seq", "chan"), P("seq", "chan"), P("chan"), P("chan", None)),
        out_specs=P("seq", "chan"),
        check_vma=False,
    )
```

```python
import functools

import jax
import jax.numpy as jnp
import ml_dtypes
import numpy as np
from jax import lax
from jax.experimental import pallas as pl
from jax.experimental.pallas import tpu as pltpu
from jax.sharding import PartitionSpec as P

MESH = pl.DeviceIdType.MESH
F32 = jnp.float32
BF16 = jnp.bfloat16
SEQ = 32
Z = 8
LANES = 128
TOK = 512
CH = 256
SEGS = TOK // LANES
HALVES = 2
CHUNK_CH = CH // HALVES
OWN = CHUNK_CH // SEQ
ROWS = OWN * SEGS
TOK_CHUNKS = 4
PIECE = TOK // TOK_CHUNKS
GROUPS = 2
GROUP = TOK // GROUPS
ORDER = (
    ("conv", 0), ("conv", 1), ("gate", 0), ("start", 0, 0), ("legs",), ("gate", 1), ("start", 1, 0), ("step", 0, 0, 0),
    ("step", 1, 0, 0), ("weights",), ("step", 0, 0, 1), ("step", 1, 0, 1), ("start", 0, 1), ("start", 1, 1),
    ("step", 0, 0, 2), ("step", 1, 0, 2), ("step", 0, 1, 0), ("step", 1, 1, 0), ("step", 0, 0, 3), ("step", 1, 0, 3),
    ("step", 0, 1, 1), ("step", 1, 1, 1), ("step", 0, 1, 2), ("step", 1, 1, 2), ("step", 0, 1, 3), ("step", 1, 1, 3),
)
SHARES = (8, 2)
WEIGHTS_FIRST = True


def tables():
    freq = (2 * np.arange(128) + 1) * np.pi / 256
    angle = np.arange(256)[:, None] * freq[None, :]
    both = np.concatenate([np.cos(angle), np.sin(angle)], axis=1)
    to_lane = both[:128]
    to_row = both[:128].T
    from_row = both[:128]
    from_lane = both.T
    return tuple(t.astype(ml_dtypes.bfloat16) for t in (to_lane, to_row, from_row, from_lane))


def dot(left, right):
    return jnp.dot(left, right, preferred_element_type=F32)


def spectrum_product(left, right):
    lcc, lcs, lsc, lss = left[:128, :128], left[:128, 128:], left[128:, :128], left[128:, 128:]
    rcc, rcs, rsc, rss = right[:128, :128], right[:128, 128:], right[128:, :128], right[128:, 128:]
    cc = lcc * rcc - lcs * rcs - lsc * rsc + lss * rss
    cs = lcc * rcs + lcs * rcc - lsc * rss - lss * rsc
    sc = lcc * rsc - lcs * rss + lsc * rcc - lss * rcs
    ss = lcc * rss + lcs * rsc + lsc * rcs + lss * rcc
    top = jnp.concatenate([cc, cs], axis=1)
    bottom = jnp.concatenate([sc, ss], axis=1)
    return jnp.concatenate([top, bottom], axis=0).astype(BF16)


def kernel(
    kv_hbm, gate_hbm, filt_hbm, skip_hbm, w_ref, to_lane_hbm, to_row_hbm, from_row_hbm, from_lane_hbm,
    out_ref,
    kv_ref, gate_ref, filt_ref, skip_ref, to_lane, to_row, from_row, from_lane, load_sem,
    spread, send_a, recv_a, rows_x, rows_h, rows_y, send_c, recv_c, rows_c,
    gated, weights_0, weights_1, acc, part_out, part_in,
    a_send, a_recv, c_send, c_recv, w1_send, w1_recv, w2_send, w2_recv, w3_send, w3_recv, w_local,
    right_send, right_recv, left_send, left_recv, y_send, y_recv,
):
    me = lax.axis_index("seq")
    chan = lax.axis_index("chan")
    y_hi = chan // Z
    z = lax.rem(chan, Z)
    core = lax.rem(me, 2)
    x = me // 8
    shares = [x * 2 + core if SHARES[half] == 8 else core for half in range(HALVES)]
    weights = (weights_0, weights_1)
    depths = [CHUNK_CH // SHARES[half] for half in range(HALVES)]

    def weight_piece(half, to, rel):
        row = half * CHUNK_CH + shares[half] * depths[half]
        column = (y_hi + rel - 2 * y_hi * rel) * Z * CH + to * CH
        return w_ref.at[
            pl.ds(pl.multiple_of(row, depths[half]), depths[half]), pl.ds(pl.multiple_of(column, CH), CH)
        ]


    def chan_of(hi, zz):
        return hi * Z + lax.rem(zz, Z)

    right, left = chan_of(y_hi, z + 1), chan_of(y_hi, z + Z - 1)
    partner = chan_of(1 - y_hi, z)
    barrier = pltpu.get_barrier_semaphore()

    def greet_seq(k, carry):
        pl.semaphore_signal(
            barrier, inc=1, device_id={"seq": lax.rem(me + k, SEQ)}, device_id_type=MESH
        )
        return carry

    def greet_z(k, carry):
        pl.semaphore_signal(
            barrier, inc=1, device_id={"chan": chan_of(y_hi, z + k)}, device_id_type=MESH
        )
        return carry

    lax.fori_loop(1, SEQ, greet_seq, 0)
    lax.fori_loop(1, Z, greet_z, 0)
    pl.semaphore_signal(barrier, inc=1, device_id={"chan": partner}, device_id_type=MESH)

    loads = [
        pltpu.make_async_copy(source, target, load_sem.at[at])
        for at, (source, target) in enumerate(
            (
                (kv_hbm, kv_ref), (filt_hbm, filt_ref), (to_lane_hbm, to_lane), (to_row_hbm, to_row),
                (from_row_hbm, from_row), (from_lane_hbm, from_lane), (gate_hbm, gate_ref), (skip_hbm, skip_ref),
            )
        )
    ]
    for load in loads:
        load.start()
    loads[0].wait()
    loads[1].wait()

    for which, source in enumerate((kv_ref, filt_ref)):
        for seg in range(SEGS):
            for part in range(CH // LANES):
                block = source[seg * LANES : (seg + 1) * LANES, part * LANES : (part + 1) * LANES]
                turned = block.astype(F32).T
                for quarter in range(LANES // SEQ):
                    index = part * (LANES // SEQ) + quarter
                    half, own = index // OWN, index % OWN
                    spread[half, pl.ds(seg * OWN + own, SEQ, stride=ROWS), :] = turned[
                        quarter * SEQ : (quarter + 1) * SEQ
                    ]
        for half in range(HALVES):
            at = (2 * half + which) * ROWS
            send_a[:, at : at + ROWS, :] = (
                spread[half].reshape(SEQ, ROWS, LANES).astype(BF16)
            )
    recv_a[me] = send_a[me]

    own_copies = [
        pltpu.make_async_copy(
            weight_piece(half, z, rel), weights[half].at[shares[half], z, rel], w_local.at[half, rel]
        )
        for half in range(HALVES)
        for rel in range(2)
    ]
    for copy in own_copies:
        copy.start()

    for load in loads[2:]:
        load.wait()
    for copy in own_copies:
        copy.wait()
    pl.semaphore_wait(barrier, SEQ - 1 + Z - 1 + 1)

    def send_signal():
        def one(k, carry):
            peer = lax.rem(me + k, SEQ)
            pltpu.make_async_remote_copy(
                src_ref=send_a.at[peer],
                dst_ref=recv_a.at[me],
                send_sem=a_send,
                recv_sem=a_recv,
                device_id={"seq": peer},
                device_id_type=MESH,
            ).start()
            return carry

        lax.fori_loop(1, SEQ, one, 0)

    def wait_bytes(ref, sem):
        pltpu.make_async_copy(ref, ref, sem).wait()

    if not WEIGHTS_FIRST:
        send_signal()
    for half in range(HALVES):

        def send_weight(k, carry, half=half):
            to = lax.rem(z + k, Z)
            for rel in range(2):
                pltpu.make_async_remote_copy(
                    src_ref=weight_piece(half, to, rel),
                    dst_ref=weights[half].at[shares[half], z, rel],
                    send_sem=w1_send.at[half],
                    recv_sem=w1_recv.at[half],
                    device_id={"chan": chan_of(y_hi, to)},
                    device_id_type=MESH,
                ).start()
            return carry

        lax.fori_loop(1, Z, send_weight, 0)
    others = pl.ds(0, SEQ - 1)
    if WEIGHTS_FIRST:
        send_signal()

    def convolve(half):
        for which, rows in enumerate((rows_x, rows_h)):
            at = (2 * half + which) * ROWS
            rows[...] = recv_a[:, at : at + ROWS, :].astype(F32).reshape(SEQ * ROWS, LANES)
        first_row = lax.broadcasted_iota(jnp.int32, (LANES, LANES), 0) == 0
        for own in range(OWN):
            spectra = []
            for rows in (rows_x, rows_h):
                blocks = rows[pl.ds(own, LANES, stride=OWN), :].astype(BF16)
                lane_freq = dot(blocks, to_lane[...]).astype(BF16)
                spectra.append(dot(to_row[...], lane_freq))
            product = spectrum_product(*spectra)
            back = dot(from_row[...], product).astype(BF16)
            wide = dot(back, from_lane[...])
            carried = jnp.where(first_row, 0.0, pltpu.roll(wide[:, LANES:], 1, 0))
            rows_y[pl.ds(own, LANES, stride=OWN), :] = (wide[:, :LANES] + carried) * (
                1.0 / (128 * 128)
            )
        send_c[half] = rows_y[...].reshape(SEQ, ROWS, LANES).astype(BF16)
        recv_c[half, me] = send_c[half, me]

    def send_back(half):
        def one(k, carry):
            peer = lax.rem(me + k, SEQ)
            pltpu.make_async_remote_copy(
                src_ref=send_c.at[half, peer],
                dst_ref=recv_c.at[half, me],
                send_sem=c_send.at[half],
                recv_sem=c_recv.at[half],
                device_id={"seq": peer},
                device_id_type=MESH,
            ).start()
            return carry

        lax.fori_loop(1, SEQ, one, 0)

    def first_leg_bytes(half):
        return weights[half].at[0, pl.ds(0, Z - 1)]

    def second_leg(half):
        if SHARES[half] == 2:
            return
        share = shares[half]

        def one(k, carry):
            pltpu.make_async_remote_copy(
                src_ref=weights[half].at[share],
                dst_ref=weights[half].at[share],
                send_sem=w2_send.at[half],
                recv_sem=w2_recv.at[half],
                device_id={"seq": lax.rem(me + 8 * k, SEQ)},
                device_id_type=MESH,
            ).start()
            return carry

        wait_bytes(first_leg_bytes(half), w1_recv.at[half])
        lax.fori_loop(1, 4, one, 0)

    def third_leg(half):
        if SHARES[half] == 2:
            wait_bytes(first_leg_bytes(half), w1_recv.at[half])
        else:
            wait_bytes(weights[half].at[pl.ds(0, 3)], w2_recv.at[half])

        def one(k, carry):
            which = 2 * k + core
            pltpu.make_async_remote_copy(
                src_ref=weights[half].at[which],
                dst_ref=weights[half].at[which],
                send_sem=w3_send.at[half],
                recv_sem=w3_recv.at[half],
                device_id={"seq": me + 1 - 2 * core},
                device_id_type=MESH,
            ).start()
            return carry

        lax.fori_loop(0, SHARES[half] // 2, one, 0)

    def third_leg_bytes(half):
        return weights[half].at[pl.ds(0, SHARES[half] // 2)]

    for half in range(HALVES):
        second_leg(half)
    def transform(half):
        if half == 0:
            wait_bytes(recv_a.at[others], a_recv)
        convolve(half)
        send_back(half)

    def piece(block, half, chunk):
        return gated.at[block, half, pl.ds(chunk * PIECE, PIECE)]

    def to_right(half, step, chunk):
        ref = piece(lax.rem(z - step + Z, Z), half, chunk)
        return pltpu.make_async_remote_copy(
            src_ref=ref,
            dst_ref=ref,
            send_sem=right_send.at[half, step, chunk],
            recv_sem=right_recv.at[half, step, chunk],
            device_id={"chan": right},
            device_id_type=MESH,
        )

    def to_left(half, step, chunk):
        ref = piece(lax.rem(z + step, Z), half, chunk)
        return pltpu.make_async_remote_copy(
            src_ref=ref,
            dst_ref=ref,
            send_sem=left_send.at[half, step, chunk],
            recv_sem=left_recv.at[half, step, chunk],
            device_id={"chan": left},
            device_id_type=MESH,
        )

    def arrive(ref, sem):
        pltpu.make_async_copy(ref, ref, sem).wait()

    def goes_right(step, chunk):
        return step < 3 or (step == 3 and chunk % 2 == 0)

    def goes_left(step, chunk):
        return step < 3 or (step == 3 and chunk % 2 == 1)

    def tokens_of(group):
        return pl.ds(group * GROUP, GROUP)

    def chunks_of(group):
        per = TOK_CHUNKS // GROUPS
        return range(group * per, (group + 1) * per)

    def add_block(block, half, group, first=False):
        tokens = tokens_of(group)
        for rel in range(2):
            weight = weights[half][:, block, rel].reshape(CHUNK_CH, CH)
            term = dot(gated[block, half, tokens], weight)
            if first:
                acc[rel, tokens] = term
            else:
                acc[rel, tokens] += term

    def gate(half):
        wait_bytes(recv_c.at[half, others], c_recv.at[half])
        rows_c[...] = recv_c[half].astype(F32).reshape(SEQ * ROWS, LANES)
        for seg in range(SEGS):
            columns = []
            for part in range(CHUNK_CH // LANES):
                per = LANES // SEQ
                stacked = jnp.concatenate(
                    [
                        rows_c[pl.ds(seg * OWN + part * per + own, SEQ, stride=ROWS), :]
                        for own in range(per)
                    ],
                    axis=0,
                )
                columns.append(stacked.T)
            conv = jnp.concatenate(columns, axis=1) if len(columns) > 1 else columns[0]
            tokens = slice(seg * LANES, (seg + 1) * LANES)
            chans = slice(half * CHUNK_CH, (half + 1) * CHUNK_CH)
            signal = kv_ref[tokens, chans].astype(F32)
            value = gate_ref[tokens, chans].astype(F32) * (conv + skip_ref[:, chans] * signal)
            gated[z, half, tokens, :] = value.astype(BF16)

    def start_group(half, group):
        for chunk in chunks_of(group):
            to_right(half, 0, chunk).start()
            to_left(half, 0, chunk).start()

    def sources(step):
        return lax.rem(z + Z - step - 1, Z), lax.rem(z + step + 1, Z)

    def pass_on(half, group, step):
        from_left, from_right = sources(step)
        for chunk in chunks_of(group):
            if goes_right(step, chunk):
                arrive(piece(from_left, half, chunk), right_recv.at[half, step, chunk])
                if goes_right(step + 1, chunk):
                    to_right(half, step + 1, chunk).start()
            if goes_left(step, chunk):
                arrive(piece(from_right, half, chunk), left_recv.at[half, step, chunk])
                if goes_left(step + 1, chunk):
                    to_left(half, step + 1, chunk).start()

    def add_step(half, group, step):
        from_left, from_right = sources(step)
        add_block(from_left, half, group)
        if step < 3:
            add_block(from_right, half, group)

    exchanges = []
    waiting = []

    def finish(half, group, step):
        add_step(half, group, step)
        if half < HALVES - 1 or step < 3:
            return
        tokens = tokens_of(group)
        part_out[tokens] = acc[1, tokens].astype(BF16)
        exchange = pltpu.make_async_remote_copy(
            src_ref=part_out.at[tokens],
            dst_ref=part_in.at[tokens],
            send_sem=y_send.at[group],
            recv_sem=y_recv.at[group],
            device_id={"chan": partner},
            device_id_type=MESH,
        )
        exchange.start()
        exchanges.append((group, exchange))

    for kind, *event in ORDER:
        if kind == "conv":
            transform(*event)
        elif kind == "start":
            start_group(*event)
        elif kind == "legs":
            for half in range(HALVES):
                third_leg(half)
        elif kind == "gate":
            gate(*event)
        elif kind == "weights":
            for half in range(HALVES):
                wait_bytes(third_leg_bytes(half), w3_recv.at[half])
            for group in range(GROUPS):
                add_block(z, 0, group, True)
                add_block(z, 1, group)
            for arrived in waiting:
                finish(*arrived)
            waiting = None
        else:
            pass_on(*event)
            if waiting is None:
                finish(*event)
            else:
                waiting.append(event)

    wait_bytes(send_a.at[others], a_send)
    for half in range(HALVES):
        wait_bytes(send_c.at[half, others], c_send.at[half])
        for step in range(4):
            for chunk in range(TOK_CHUNKS):
                if goes_right(step, chunk):
                    arrive(piece(0, half, chunk), right_send.at[half, step, chunk])
                if goes_left(step, chunk):
                    arrive(piece(0, half, chunk), left_send.at[half, step, chunk])
    for half in range(HALVES):
        wait_bytes(first_leg_bytes(half), w1_send.at[half])
        if SHARES[half] == 8:
            wait_bytes(weights[half].at[pl.ds(0, 3)], w2_send.at[half])
        wait_bytes(third_leg_bytes(half), w3_send.at[half])
    for group, exchange in exchanges:
        tokens = tokens_of(group)
        exchange.wait()
        out_ref[tokens] = (acc[0, tokens] + part_in[tokens].astype(F32)).astype(BF16)


def per_device(key_value, gating, long_filter, skip_gain, out_weight):
    vmem = pl.BlockSpec(memory_space=pltpu.VMEM)
    anywhere = pl.BlockSpec(memory_space=pl.ANY)
    dma = pltpu.SemaphoreType.DMA
    ring = dma((HALVES, 4, TOK_CHUNKS))
    return pl.pallas_call(
        kernel,
        out_shape=jax.ShapeDtypeStruct((TOK, CH), BF16),
        in_specs=[anywhere] * 9,
        out_specs=vmem,
        scratch_shapes=[
            pltpu.VMEM((TOK, CH), BF16),
            pltpu.VMEM((TOK, CH), BF16),
            pltpu.VMEM((TOK, CH), BF16),
            pltpu.VMEM((1, CH), F32),
            pltpu.VMEM((128, 256), BF16),
            pltpu.VMEM((256, 128), BF16),
            pltpu.VMEM((128, 256), BF16),
            pltpu.VMEM((256, 256), BF16),
            dma((8,)),
            pltpu.VMEM((HALVES, SEQ * ROWS, LANES), F32),
            pltpu.VMEM((SEQ, HALVES * 2 * ROWS, LANES), BF16),
            pltpu.VMEM((SEQ, HALVES * 2 * ROWS, LANES), BF16),
            pltpu.VMEM((SEQ * ROWS, LANES), F32),
            pltpu.VMEM((SEQ * ROWS, LANES), F32),
            pltpu.VMEM((SEQ * ROWS, LANES), F32),
            pltpu.VMEM((HALVES, SEQ, ROWS, LANES), BF16),
            pltpu.VMEM((HALVES, SEQ, ROWS, LANES), BF16),
            pltpu.VMEM((SEQ * ROWS, LANES), F32),
            pltpu.VMEM((Z, HALVES, TOK, CHUNK_CH), BF16),
            *(pltpu.VMEM((count, Z, 2, CHUNK_CH // count, CH), BF16) for count in SHARES),
            pltpu.VMEM((2, TOK, CH), F32),
            pltpu.VMEM((TOK, CH), BF16),
            pltpu.VMEM((TOK, CH), BF16),
            dma, dma, dma((HALVES,)), dma((HALVES,)),
            *(dma((HALVES,)) for _ in range(6)), dma((HALVES, 2)),
            ring, ring, ring, ring,
            dma((GROUPS,)), dma((GROUPS,)),
        ],
        compiler_params=pltpu.CompilerParams(
            collective_id=0, has_side_effects=True, vmem_limit_bytes=60 * 2**20
        ),
    )(
        key_value, gating, long_filter, skip_gain.reshape(1, CH), out_weight,
        *(jnp.asarray(t) for t in tables()),
    )


def solution(mesh):
    return jax.shard_map(
        per_device,
        mesh=mesh,
        in_specs=(P("seq", "chan"), P("seq", "chan"), P("seq", "chan"), P("chan"), P("chan", None)),
        out_specs=P("seq", "chan"),
        check_vma=False,
    )
```

```python
import functools

import jax
import jax.numpy as jnp
import ml_dtypes
import numpy as np
from jax import lax
from jax.experimental import pallas as pl
from jax.experimental.pallas import tpu as pltpu
from jax.sharding import PartitionSpec as P

MESH = pl.DeviceIdType.MESH
F32 = jnp.float32
BF16 = jnp.bfloat16
SEQ = 32
Z = 8
LANES = 128
TOK = 512
CH = 256
SEGS = TOK // LANES
HALVES = 2
CHUNK_CH = CH // HALVES
OWN = CHUNK_CH // SEQ
ROWS = OWN * SEGS
TOK_CHUNKS = 4
PIECE = TOK // TOK_CHUNKS
GROUPS = 2
FIRST = 3
ORDER = (
    ("conv", 0), ("conv", 1), ("gate", 0), ("start", 0, 0), ("legs",), ("gate", 1), ("start", 1, 0), ("step", 0, 0, 0),
    ("step", 1, 0, 0), ("weights",), ("step", 0, 0, 1), ("step", 1, 0, 1), ("start", 0, 1), ("start", 1, 1),
    ("step", 0, 0, 2), ("step", 1, 0, 2), ("step", 0, 1, 0), ("step", 1, 1, 0), ("step", 0, 0, 3), ("step", 1, 0, 3),
    ("step", 0, 1, 1), ("step", 1, 1, 1), ("step", 0, 1, 2), ("step", 1, 1, 2), ("step", 0, 1, 3), ("step", 1, 1, 3),
)
SHARES = (8, 2)
WEIGHTS_FIRST = True


def tables():
    freq = (2 * np.arange(128) + 1) * np.pi / 256
    angle = np.arange(256)[:, None] * freq[None, :]
    both = np.concatenate([np.cos(angle), np.sin(angle)], axis=1)
    to_lane = both[:128]
    to_row = both[:128].T
    from_row = both[:128]
    from_lane = both.T
    return tuple(t.astype(ml_dtypes.bfloat16) for t in (to_lane, to_row, from_row, from_lane))


def dot(left, right):
    return jnp.dot(left, right, preferred_element_type=F32)


def spectrum_product(left, right):
    lcc, lcs, lsc, lss = left[:128, :128], left[:128, 128:], left[128:, :128], left[128:, 128:]
    rcc, rcs, rsc, rss = right[:128, :128], right[:128, 128:], right[128:, :128], right[128:, 128:]
    cc = lcc * rcc - lcs * rcs - lsc * rsc + lss * rss
    cs = lcc * rcs + lcs * rcc - lsc * rss - lss * rsc
    sc = lcc * rsc - lcs * rss + lsc * rcc - lss * rcs
    ss = lcc * rss + lcs * rsc + lsc * rcs + lss * rcc
    top = jnp.concatenate([cc, cs], axis=1)
    bottom = jnp.concatenate([sc, ss], axis=1)
    return jnp.concatenate([top, bottom], axis=0).astype(BF16)


def kernel(
    kv_hbm, gate_hbm, filt_hbm, skip_hbm, w_ref, to_lane_hbm, to_row_hbm, from_row_hbm, from_lane_hbm,
    out_ref,
    kv_ref, gate_ref, filt_ref, skip_ref, to_lane, to_row, from_row, from_lane, load_sem,
    spread, send_a, recv_a, rows_x, rows_h, rows_y, send_c, recv_c, rows_c,
    gated, weights_0, weights_1, acc, part_out, part_in,
    a_send, a_recv, c_send, c_recv, w1_send, w1_recv, w2_send, w2_recv, w3_send, w3_recv, w_local,
    right_send, right_recv, left_send, left_recv, y_send, y_recv,
):
    me = lax.axis_index("seq")
    chan = lax.axis_index("chan")
    y_hi = chan // Z
    z = lax.rem(chan, Z)
    core = lax.rem(me, 2)
    x = me // 8
    shares = [x * 2 + core if SHARES[half] == 8 else core for half in range(HALVES)]
    weights = (weights_0, weights_1)
    depths = [CHUNK_CH // SHARES[half] for half in range(HALVES)]

    def weight_piece(half, to, rel):
        row = half * CHUNK_CH + shares[half] * depths[half]
        column = (y_hi + rel - 2 * y_hi * rel) * Z * CH + to * CH
        return w_ref.at[
            pl.ds(pl.multiple_of(row, depths[half]), depths[half]), pl.ds(pl.multiple_of(column, CH), CH)
        ]


    def chan_of(hi, zz):
        return hi * Z + lax.rem(zz, Z)

    right, left = chan_of(y_hi, z + 1), chan_of(y_hi, z + Z - 1)
    partner = chan_of(1 - y_hi, z)
    barrier = pltpu.get_barrier_semaphore()

    def greet_seq(k, carry):
        pl.semaphore_signal(
            barrier, inc=1, device_id={"seq": lax.rem(me + k, SEQ)}, device_id_type=MESH
        )
        return carry

    def greet_z(k, carry):
        pl.semaphore_signal(
            barrier, inc=1, device_id={"chan": chan_of(y_hi, z + k)}, device_id_type=MESH
        )
        return carry

    lax.fori_loop(1, SEQ, greet_seq, 0)
    lax.fori_loop(1, Z, greet_z, 0)
    pl.semaphore_signal(barrier, inc=1, device_id={"chan": partner}, device_id_type=MESH)

    loads = [
        pltpu.make_async_copy(source, target, load_sem.at[at])
        for at, (source, target) in enumerate(
            (
                (kv_hbm, kv_ref), (filt_hbm, filt_ref), (to_lane_hbm, to_lane), (to_row_hbm, to_row),
                (from_row_hbm, from_row), (from_lane_hbm, from_lane), (gate_hbm, gate_ref), (skip_hbm, skip_ref),
            )
        )
    ]
    for load in loads:
        load.start()
    loads[0].wait()
    loads[1].wait()

    for which, source in enumerate((kv_ref, filt_ref)):
        for seg in range(SEGS):
            for part in range(CH // LANES):
                block = source[seg * LANES : (seg + 1) * LANES, part * LANES : (part + 1) * LANES]
                turned = block.astype(F32).T
                for quarter in range(LANES // SEQ):
                    index = part * (LANES // SEQ) + quarter
                    half, own = index // OWN, index % OWN
                    spread[half, pl.ds(seg * OWN + own, SEQ, stride=ROWS), :] = turned[
                        quarter * SEQ : (quarter + 1) * SEQ
                    ]
        for half in range(HALVES):
            at = (2 * half + which) * ROWS
            send_a[:, at : at + ROWS, :] = (
                spread[half].reshape(SEQ, ROWS, LANES).astype(BF16)
            )
    recv_a[me] = send_a[me]

    own_copies = [
        pltpu.make_async_copy(
            weight_piece(half, z, rel), weights[half].at[shares[half], z, rel], w_local.at[half, rel]
        )
        for half in range(HALVES)
        for rel in range(2)
    ]
    for copy in own_copies:
        copy.start()

    for load in loads[2:]:
        load.wait()
    for copy in own_copies:
        copy.wait()
    pl.semaphore_wait(barrier, SEQ - 1 + Z - 1 + 1)

    def send_signal():
        def one(k, carry):
            peer = lax.rem(me + k, SEQ)
            pltpu.make_async_remote_copy(
                src_ref=send_a.at[peer],
                dst_ref=recv_a.at[me],
                send_sem=a_send,
                recv_sem=a_recv,
                device_id={"seq": peer},
                device_id_type=MESH,
            ).start()
            return carry

        lax.fori_loop(1, SEQ, one, 0)

    def wait_bytes(ref, sem):
        pltpu.make_async_copy(ref, ref, sem).wait()

    if not WEIGHTS_FIRST:
        send_signal()
    for half in range(HALVES):

        def send_weight(k, carry, half=half):
            to = lax.rem(z + k, Z)
            for rel in range(2):
                pltpu.make_async_remote_copy(
                    src_ref=weight_piece(half, to, rel),
                    dst_ref=weights[half].at[shares[half], z, rel],
                    send_sem=w1_send.at[half],
                    recv_sem=w1_recv.at[half],
                    device_id={"chan": chan_of(y_hi, to)},
                    device_id_type=MESH,
                ).start()
            return carry

        lax.fori_loop(1, Z, send_weight, 0)
    others = pl.ds(0, SEQ - 1)
    if WEIGHTS_FIRST:
        send_signal()

    def convolve(half):
        for which, rows in enumerate((rows_x, rows_h)):
            at = (2 * half + which) * ROWS
            rows[...] = recv_a[:, at : at + ROWS, :].astype(F32).reshape(SEQ * ROWS, LANES)
        first_row = lax.broadcasted_iota(jnp.int32, (LANES, LANES), 0) == 0
        for own in range(OWN):
            spectra = []
            for rows in (rows_x, rows_h):
                blocks = rows[pl.ds(own, LANES, stride=OWN), :].astype(BF16)
                lane_freq = dot(blocks, to_lane[...]).astype(BF16)
                spectra.append(dot(to_row[...], lane_freq))
            product = spectrum_product(*spectra)
            back = dot(from_row[...], product).astype(BF16)
            wide = dot(back, from_lane[...])
            carried = jnp.where(first_row, 0.0, pltpu.roll(wide[:, LANES:], 1, 0))
            rows_y[pl.ds(own, LANES, stride=OWN), :] = (wide[:, :LANES] + carried) * (
                1.0 / (128 * 128)
            )
        send_c[half] = rows_y[...].reshape(SEQ, ROWS, LANES).astype(BF16)
        recv_c[half, me] = send_c[half, me]

    def send_back(half):
        def one(k, carry):
            peer = lax.rem(me + k, SEQ)
            pltpu.make_async_remote_copy(
                src_ref=send_c.at[half, peer],
                dst_ref=recv_c.at[half, me],
                send_sem=c_send.at[half],
                recv_sem=c_recv.at[half],
                device_id={"seq": peer},
                device_id_type=MESH,
            ).start()
            return carry

        lax.fori_loop(1, SEQ, one, 0)

    def first_leg_bytes(half):
        return weights[half].at[0, pl.ds(0, Z - 1)]

    def second_leg(half):
        if SHARES[half] == 2:
            return
        share = shares[half]

        def one(k, carry):
            pltpu.make_async_remote_copy(
                src_ref=weights[half].at[share],
                dst_ref=weights[half].at[share],
                send_sem=w2_send.at[half],
                recv_sem=w2_recv.at[half],
                device_id={"seq": lax.rem(me + 8 * k, SEQ)},
                device_id_type=MESH,
            ).start()
            return carry

        wait_bytes(first_leg_bytes(half), w1_recv.at[half])
        lax.fori_loop(1, 4, one, 0)

    def third_leg(half):
        if SHARES[half] == 2:
            wait_bytes(first_leg_bytes(half), w1_recv.at[half])
        else:
            wait_bytes(weights[half].at[pl.ds(0, 3)], w2_recv.at[half])

        def one(k, carry):
            which = 2 * k + core
            pltpu.make_async_remote_copy(
                src_ref=weights[half].at[which],
                dst_ref=weights[half].at[which],
                send_sem=w3_send.at[half],
                recv_sem=w3_recv.at[half],
                device_id={"seq": me + 1 - 2 * core},
                device_id_type=MESH,
            ).start()
            return carry

        lax.fori_loop(0, SHARES[half] // 2, one, 0)

    def third_leg_bytes(half):
        return weights[half].at[pl.ds(0, SHARES[half] // 2)]

    for half in range(HALVES):
        second_leg(half)
    def transform(half):
        if half == 0:
            wait_bytes(recv_a.at[others], a_recv)
        convolve(half)
        send_back(half)

    def piece(block, half, chunk):
        return gated.at[block, half, pl.ds(chunk * PIECE, PIECE)]

    def to_right(half, step, chunk):
        ref = piece(lax.rem(z - step + Z, Z), half, chunk)
        return pltpu.make_async_remote_copy(
            src_ref=ref,
            dst_ref=ref,
            send_sem=right_send.at[half, step, chunk],
            recv_sem=right_recv.at[half, step, chunk],
            device_id={"chan": right},
            device_id_type=MESH,
        )

    def to_left(half, step, chunk):
        ref = piece(lax.rem(z + step, Z), half, chunk)
        return pltpu.make_async_remote_copy(
            src_ref=ref,
            dst_ref=ref,
            send_sem=left_send.at[half, step, chunk],
            recv_sem=left_recv.at[half, step, chunk],
            device_id={"chan": left},
            device_id_type=MESH,
        )

    def arrive(ref, sem):
        pltpu.make_async_copy(ref, ref, sem).wait()

    def goes_right(step, chunk):
        return step < 3 or (step == 3 and chunk % 2 == 0)

    def goes_left(step, chunk):
        return step < 3 or (step == 3 and chunk % 2 == 1)

    def chunks_of(group):
        return range(FIRST) if group == 0 else range(FIRST, TOK_CHUNKS)

    def tokens_of(group):
        chunks = chunks_of(group)
        return pl.ds(chunks[0] * PIECE, len(chunks) * PIECE)

    def add_block(block, half, group, first=False):
        tokens = tokens_of(group)
        for rel in range(2):
            weight = weights[half][:, block, rel].reshape(CHUNK_CH, CH)
            term = dot(gated[block, half, tokens], weight)
            if first:
                acc[rel, tokens] = term
            else:
                acc[rel, tokens] += term

    def gate(half):
        wait_bytes(recv_c.at[half, others], c_recv.at[half])
        rows_c[...] = recv_c[half].astype(F32).reshape(SEQ * ROWS, LANES)
        for seg in range(SEGS):
            columns = []
            for part in range(CHUNK_CH // LANES):
                per = LANES // SEQ
                stacked = jnp.concatenate(
                    [
                        rows_c[pl.ds(seg * OWN + part * per + own, SEQ, stride=ROWS), :]
                        for own in range(per)
                    ],
                    axis=0,
                )
                columns.append(stacked.T)
            conv = jnp.concatenate(columns, axis=1) if len(columns) > 1 else columns[0]
            tokens = slice(seg * LANES, (seg + 1) * LANES)
            chans = slice(half * CHUNK_CH, (half + 1) * CHUNK_CH)
            signal = kv_ref[tokens, chans].astype(F32)
            value = gate_ref[tokens, chans].astype(F32) * (conv + skip_ref[:, chans] * signal)
            gated[z, half, tokens, :] = value.astype(BF16)

    def start_group(half, group):
        for chunk in chunks_of(group):
            to_right(half, 0, chunk).start()
            to_left(half, 0, chunk).start()

    def sources(step):
        return lax.rem(z + Z - step - 1, Z), lax.rem(z + step + 1, Z)

    def pass_on(half, group, step):
        from_left, from_right = sources(step)
        for chunk in chunks_of(group):
            if goes_right(step, chunk):
                arrive(piece(from_left, half, chunk), right_recv.at[half, step, chunk])
                if goes_right(step + 1, chunk):
                    to_right(half, step + 1, chunk).start()
            if goes_left(step, chunk):
                arrive(piece(from_right, half, chunk), left_recv.at[half, step, chunk])
                if goes_left(step + 1, chunk):
                    to_left(half, step + 1, chunk).start()

    def add_step(half, group, step):
        from_left, from_right = sources(step)
        add_block(from_left, half, group)
        if step < 3:
            add_block(from_right, half, group)

    exchanges = []
    waiting = []

    def finish(half, group, step):
        add_step(half, group, step)
        if half < HALVES - 1 or step < 3:
            return
        tokens = tokens_of(group)
        part_out[tokens] = acc[1, tokens].astype(BF16)
        exchange = pltpu.make_async_remote_copy(
            src_ref=part_out.at[tokens],
            dst_ref=part_in.at[tokens],
            send_sem=y_send.at[group],
            recv_sem=y_recv.at[group],
            device_id={"chan": partner},
            device_id_type=MESH,
        )
        exchange.start()
        exchanges.append((group, exchange))

    for kind, *event in ORDER:
        if kind == "conv":
            transform(*event)
        elif kind == "start":
            start_group(*event)
        elif kind == "legs":
            for half in range(HALVES):
                third_leg(half)
        elif kind == "gate":
            gate(*event)
        elif kind == "weights":
            for half in range(HALVES):
                wait_bytes(third_leg_bytes(half), w3_recv.at[half])
            for group in range(GROUPS):
                add_block(z, 0, group, True)
                add_block(z, 1, group)
            for arrived in waiting:
                finish(*arrived)
            waiting = None
        else:
            pass_on(*event)
            if waiting is None:
                finish(*event)
            else:
                waiting.append(event)

    wait_bytes(send_a.at[others], a_send)
    for half in range(HALVES):
        wait_bytes(send_c.at[half, others], c_send.at[half])
        for step in range(4):
            for chunk in range(TOK_CHUNKS):
                if goes_right(step, chunk):
                    arrive(piece(0, half, chunk), right_send.at[half, step, chunk])
                if goes_left(step, chunk):
                    arrive(piece(0, half, chunk), left_send.at[half, step, chunk])
    for half in range(HALVES):
        wait_bytes(first_leg_bytes(half), w1_send.at[half])
        if SHARES[half] == 8:
            wait_bytes(weights[half].at[pl.ds(0, 3)], w2_send.at[half])
        wait_bytes(third_leg_bytes(half), w3_send.at[half])
    for group, exchange in exchanges:
        tokens = tokens_of(group)
        exchange.wait()
        out_ref[tokens] = (acc[0, tokens] + part_in[tokens].astype(F32)).astype(BF16)


def per_device(key_value, gating, long_filter, skip_gain, out_weight):
    vmem = pl.BlockSpec(memory_space=pltpu.VMEM)
    anywhere = pl.BlockSpec(memory_space=pl.ANY)
    dma = pltpu.SemaphoreType.DMA
    ring = dma((HALVES, 4, TOK_CHUNKS))
    return pl.pallas_call(
        kernel,
        out_shape=jax.ShapeDtypeStruct((TOK, CH), BF16),
        in_specs=[anywhere] * 9,
        out_specs=vmem,
        scratch_shapes=[
            pltpu.VMEM((TOK, CH), BF16),
            pltpu.VMEM((TOK, CH), BF16),
            pltpu.VMEM((TOK, CH), BF16),
            pltpu.VMEM((1, CH), F32),
            pltpu.VMEM((128, 256), BF16),
            pltpu.VMEM((256, 128), BF16),
            pltpu.VMEM((128, 256), BF16),
            pltpu.VMEM((256, 256), BF16),
            dma((8,)),
            pltpu.VMEM((HALVES, SEQ * ROWS, LANES), F32),
            pltpu.VMEM((SEQ, HALVES * 2 * ROWS, LANES), BF16),
            pltpu.VMEM((SEQ, HALVES * 2 * ROWS, LANES), BF16),
            pltpu.VMEM((SEQ * ROWS, LANES), F32),
            pltpu.VMEM((SEQ * ROWS, LANES), F32),
            pltpu.VMEM((SEQ * ROWS, LANES), F32),
            pltpu.VMEM((HALVES, SEQ, ROWS, LANES), BF16),
            pltpu.VMEM((HALVES, SEQ, ROWS, LANES), BF16),
            pltpu.VMEM((SEQ * ROWS, LANES), F32),
            pltpu.VMEM((Z, HALVES, TOK, CHUNK_CH), BF16),
            *(pltpu.VMEM((count, Z, 2, CHUNK_CH // count, CH), BF16) for count in SHARES),
            pltpu.VMEM((2, TOK, CH), F32),
            pltpu.VMEM((TOK, CH), BF16),
            pltpu.VMEM((TOK, CH), BF16),
            dma, dma, dma((HALVES,)), dma((HALVES,)),
            *(dma((HALVES,)) for _ in range(6)), dma((HALVES, 2)),
            ring, ring, ring, ring,
            dma((GROUPS,)), dma((GROUPS,)),
        ],
        compiler_params=pltpu.CompilerParams(
            collective_id=0, has_side_effects=True, vmem_limit_bytes=60 * 2**20
        ),
    )(
        key_value, gating, long_filter, skip_gain.reshape(1, CH), out_weight,
        *(jnp.asarray(t) for t in tables()),
    )


def solution(mesh):
    return jax.shard_map(
        per_device,
        mesh=mesh,
        in_specs=(P("seq", "chan"), P("seq", "chan"), P("seq", "chan"), P("chan"), P("chan", None)),
        out_specs=P("seq", "chan"),
        check_vma=False,
    )
```
